256 devices in a mesh: seq: 64 (over x, z, core), head: 4 (over y).
Axes of the slice: x: 4, y: 4, z: 8, core: 2. Of those that a mesh axis runs over, the one named last changes fastest.
Arguments:
- queries: bfloat16 [49152, 4096], P('seq', 'head')
- keys: bfloat16 [49152, 4096], P('seq', 'head'), may hold values from -4 to 4
- values: bfloat16 [49152, 4096], P('seq', 'head')
- cotangent: bfloat16 [49152, 4096], P('seq', 'head'), may hold values from -6 to 6
- norm_gain: float32 [4096], P('head'), may hold values from 0.1 to 1.9
- doc_start: int32 [49152], P('seq'), may hold values from 0 to 48896, as said below
Outputs:
- normed: bfloat16 [49152, 4096], P('seq', 'head')
- grad_queries: bfloat16 [49152, 4096], P('seq', 'head')
- grad_keys: bfloat16 [49152, 4096], P('seq', 'head')
- grad_values: bfloat16 [49152, 4096], P('seq', 'head')
The draws below stay inside these ranges and needn't reach their ends.
Inputs may be any that keep to these rules, and one draw needn't show every extreme that they name: doc_start[t] is the start of t's document: a multiple of 256, at most t, equal for all tokens of a document, and equal to t at each document's first token. Every document touches at most 16 consecutive blocks of 768 tokens, and in every draw some document touches exactly 16 blocks. The last 256 tokens form a document of their own.
All inputs are finite; a program needn't handle non-finite values.
Results may differ from the reference program's by a relative error of at most 0.0058.
Values sent between devices are 32-bit elements; how exact they have to be, the bound alone decides.
No kernel may reach another device: no remote copies, remote signals or barrier semaphores. Data moves between devices by JAX's collectives and lax.ppermute only.
A program may use at most 192 MiB of HBM per device.

```python
import math
import jax
import jax.numpy as jnp
from jax import lax

HEADS = 32
HEAD_DIM = 128
TOK_DEV = 768
UNIT = 256
SPAN_DEV = 16
TOKENS = 49152
FEATURES = 4096


def draw_queries(key, part):
    base_key, row_key = jax.random.split(key)
    base_draw = jax.random.normal(base_key, (TOKENS, HEADS * HEAD_DIM), jnp.float32)
    scales = jnp.exp(jax.random.uniform(row_key, (TOKENS, 1), jnp.float32, 0.0, math.log(10.0))) / math.sqrt(10.0)
    return (base_draw * scales * HEAD_DIM ** (-0.25)).astype(jnp.bfloat16)


def draw_values(key, part):
    base_key, column_key = jax.random.split(key, 2)
    features = HEADS * HEAD_DIM
    head_trend = (jnp.arange(features) // HEAD_DIM).astype(jnp.float32) / max(HEADS - 1, 1)
    spread = jax.random.uniform(column_key, (1, features), jnp.float32)
    columns = jnp.exp(math.log(10.0) * 0.5 * (head_trend[None, :] + spread)) / math.sqrt(10.0)
    base_draw = jax.random.normal(base_key, (TOKENS, features), jnp.float32)
    return (base_draw * columns).astype(jnp.bfloat16)


def draw_doc_start(key, part):
    unit_count = TOKENS // UNIT
    per_block = TOK_DEV // UNIT
    block_count = TOKENS // TOK_DEV
    group_units = SPAN_DEV * per_block
    cut_key, place_key, head_key, tail_key = jax.random.split(key, 4)
    lowest = max(0, block_count // 2 + 2 - SPAN_DEV)
    highest = block_count // 2 - 1
    first_block = jax.random.randint(place_key, (), lowest, highest + 1).astype(jnp.int32)
    open_unit = first_block * per_block + jax.random.randint(head_key, (), 0, per_block).astype(jnp.int32)
    close_unit = (first_block + SPAN_DEV - 1) * per_block + jax.random.randint(tail_key, (), 1, per_block + 1).astype(jnp.int32)
    unit_index = jnp.arange(unit_count, dtype=jnp.int32)
    random_cut = jax.random.randint(cut_key, (unit_count,), 0, 3) == 0
    inside = (unit_index > open_unit) & (unit_index < close_unit)
    free_cut = (unit_index % group_units == 0) | random_cut
    starts_here = (unit_index == 0) | (unit_index == open_unit) | (unit_index == close_unit) | (unit_index == unit_count - 1) | free_cut & jnp.logical_not(inside)
    start_token = jnp.where(starts_here, unit_index * UNIT, 0).astype(jnp.int32)
    start_token = lax.cummax(start_token, axis=0)
    return jnp.repeat(start_token, UNIT, total_repeat_length=TOKENS).astype(jnp.int32)


def level_of(rng, extent, cuts, low, largest):
    def one(dim, shards_of):
        heights = jax.random.uniform(jax.random.fold_in(jax.random.fold_in(rng, 6), dim), (shards_of,), jnp.float32, low / len(cuts), largest / len(cuts))
        return jnp.repeat(jnp.exp(heights), extent[dim] // shards_of).reshape((-1,) + (1,) * (len(extent) - dim - 1))

    gain = one(*cuts[0])
    for cut in cuts[1:]:
        gain = gain * one(*cut)
    return gain


def bell_draw(key, shape, deviation, bound, shards=(), kind=jnp.bfloat16):
    entries = jax.random.normal(key, shape, jnp.float32) * deviation
    if len(shards) > 0:
        entries = level_of(key, shape, shards, -0.22, 0.18) * entries
    return jnp.clip(entries, min=-bound, max=bound).astype(kind)


def setup_inputs(seed: int = 0) -> dict:
    key_of = jax.random.split(jax.random.key(seed), 7)
    queries = draw_queries(jax.random.fold_in(key_of[6], 71), 0)
    keys = bell_draw(key_of[1], (TOKENS, FEATURES), (HEAD_DIM ** -0.25), 4.0, ((0, 64), (1, 4)))
    values = draw_values(jax.random.fold_in(key_of[6], 71), 0)
    cotangent = bell_draw(key_of[3], (TOKENS, FEATURES), 1.0, 6.0, ((0, 64), (1, 4)))
    norm_gain = jnp.clip(1.0 + 0.18 * jax.random.normal(key_of[4], (FEATURES,), jnp.float32), 0.1, 1.9)
    doc_start = draw_doc_start(jax.random.fold_in(key_of[6], 71), 0)
    return {"queries": queries, "keys": keys, "values": values, "cotangent": cotangent, "norm_gain": norm_gain, "doc_start": doc_start}


epsilon = 1e-06

def product(form, left, right):
    return jnp.einsum(form, left.astype(jnp.float32), right.astype(jnp.float32), precision=lax.Precision.HIGHEST)

def reference(queries, keys, values, cotangent, norm_gain, doc_start):
    blocks = TOKENS // TOK_DEV
    features = HEADS * HEAD_DIM

    def split(data):
        return data.reshape(blocks, TOK_DEV, HEADS, HEAD_DIM)
    block_docs = doc_start.reshape(blocks, TOK_DEV)
    offsets = (jnp.arange(blocks, dtype=jnp.int32) * TOK_DEV).astype(jnp.int32)
    position = jnp.arange(TOK_DEV, dtype=jnp.int32)

    def block_masks(doc, offset):
        same_doc = (doc[:, None] == doc[None, :]) & (position[:, None] >= position[None, :])
        begins = jnp.any(doc == offset + position)
        return (same_doc, begins, doc < offset, doc == doc[-1])

    def forward(carry, inputs):
        query, key, value, grad_y, doc, offset = inputs
        same_doc, begins, carried, closing = block_masks(doc, offset)
        attend = jnp.where(same_doc[None], product('thd,shd->hts', query, key), 0.0).astype(jnp.bfloat16)
        prefix = carry.astype(jnp.bfloat16)
        attended = product('hts,she->the', attend, value) + jnp.where(carried[:, None, None], product('thd,hde->the', query, prefix), 0.0)
        flat_out = attended.reshape(TOK_DEV, features)
        scaled = norm_gain[None, :] * grad_y.reshape(TOK_DEV, features).astype(jnp.float32)
        inverse = lax.rsqrt(lax.optimization_barrier(jnp.sum(flat_out * flat_out, axis=1)) / features + epsilon)
        cross = lax.optimization_barrier(jnp.sum(scaled * flat_out, axis=1))
        normed = (flat_out * inverse[:, None] * norm_gain[None, :]).astype(jnp.bfloat16)
        grad_flat = inverse[:, None] * (scaled - flat_out * (inverse * inverse * cross / features)[:, None])
        grad_out = grad_flat.astype(jnp.bfloat16).reshape(TOK_DEV, HEADS, HEAD_DIM)
        backs = jnp.where(same_doc[None], product('the,she->hts', grad_out, value), 0.0).astype(jnp.bfloat16)
        grad_q = product('hts,shd->thd', backs, key) + jnp.where(carried[:, None, None], product('the,hde->thd', grad_out, prefix), 0.0)
        tail_state = product('thd,the->hde', jnp.where(closing[:, None, None], key, 0), value)
        updated = tail_state + jnp.where(begins, 0.0, 1.0) * carry
        return (updated, (normed, grad_q.astype(jnp.bfloat16), grad_out))
    zero_state = jnp.zeros((HEADS, HEAD_DIM, HEAD_DIM), jnp.float32)
    _, (normed, grad_q, grad_out) = lax.scan(forward, zero_state, (split(queries), split(keys), split(values), split(cotangent), block_docs, offsets))

    def backward(carry, inputs):
        query, key, value, grad_part, doc, offset = inputs
        same_doc, begins, carried, closing = block_masks(doc, offset)
        attend = jnp.where(same_doc[None], product('thd,shd->hts', query, key), 0.0).astype(jnp.bfloat16)
        backs = jnp.where(same_doc[None], product('the,she->hts', grad_part, value), 0.0).astype(jnp.bfloat16)
        after_bf = carry.astype(jnp.bfloat16)
        grad_k = product('hts,thd->shd', backs, query) + jnp.where(closing[:, None, None], product('she,hde->shd', value, after_bf), 0.0)
        grad_v = product('hts,the->she', attend, grad_part) + jnp.where(closing[:, None, None], product('shd,hde->she', key, after_bf), 0.0)
        head_state = product('thd,the->hde', jnp.where(carried[:, None, None], query, 0), grad_part)
        updated = head_state + jnp.where(begins, 0.0, 1.0) * carry
        return (updated, (grad_k.astype(jnp.bfloat16), grad_v.astype(jnp.bfloat16)))
    _, (grad_k, grad_v) = lax.scan(backward, zero_state, (split(queries), split(keys), split(values), grad_out, block_docs, offsets), reverse=True)
    return (normed.reshape(TOKENS, features), grad_q.reshape(TOKENS, features), grad_k.reshape(TOKENS, features), grad_v.reshape(TOKENS, features))
```

```python
import functools

import jax
import jax.numpy as jnp
from jax import lax
from jax.experimental import pallas as pl
from jax.experimental.pallas import tpu as pltpu
from jax.sharding import PartitionSpec as P

HEAD_DIM = 128
UNIT = 256
SLICE = 16
epsilon = 1e-06

F32 = jnp.float32
BF16 = jnp.bfloat16


def dot(left, right, contract):
    return lax.dot_general(
        left, right, ((contract[0:1], contract[1:2]), ((), ())), preferred_element_type=F32
    )


def unit(index):
    return slice(index * UNIT, (index + 1) * UNIT)


def columns(index):
    return slice(index * HEAD_DIM, (index + 1) * HEAD_DIM)


def causal():
    rows = lax.broadcasted_iota(jnp.int32, (UNIT, UNIT), 0)
    return rows >= lax.broadcasted_iota(jnp.int32, (UNIT, UNIT), 1)


def tile_mask(doc_ref, later, earlier):
    if later == earlier:
        return causal()
    return jnp.full((UNIT, UNIT), doc_ref[later * UNIT] == doc_ref[earlier * UNIT])


def masked_rows(keep, rows):
    return jnp.where(jnp.full(rows.shape, keep), rows, jnp.zeros_like(rows))


def column_of(row):
    return jnp.transpose(jnp.broadcast_to(row, (HEAD_DIM, row.shape[1])))


def tail_kernel(heads, doc_ref, key_ref, value_ref, state_ref):
    tokens = key_ref.shape[0]
    units = tokens // UNIT
    last = doc_ref[tokens - 1]
    parts = HEAD_DIM // SLICE
    for h in range(heads):
        total = jnp.zeros((HEAD_DIM, HEAD_DIM), F32)
        for u in range(units):
            key = masked_rows(doc_ref[u * UNIT] == last, key_ref[unit(u), columns(h)])
            total += dot(key, value_ref[unit(u), columns(h)], (0, 0))
        state_ref[h * parts : (h + 1) * parts, 0:SLICE, :] = total.reshape(parts, SLICE, HEAD_DIM)
    offset = lax.axis_index("seq") * tokens
    flag = jnp.where(last >= offset, 0.0, 1.0).astype(F32)
    state_ref[:, SLICE:, :] = jnp.full((state_ref.shape[0], 8, HEAD_DIM), flag)


def scan_kernel(reverse, part_ref, flag_ref, state_ref):
    count = part_ref.shape[0]
    carry = jnp.zeros((SLICE, HEAD_DIM), F32)
    for step in range(count):
        b = count - 1 - step if reverse else step
        state_ref[b] = carry
        carry = part_ref[b, 0:SLICE, :] + flag_ref[b, 0:1, :] * carry


def local_kernel(heads, doc_ref, query_ref, key_ref, value_ref, out_ref):
    units = query_ref.shape[0] // UNIT
    for h in range(heads):
        for t in range(units):
            total = jnp.zeros((UNIT, HEAD_DIM), F32)
            for s in range(t + 1):
                score = dot(query_ref[unit(t), columns(h)], key_ref[unit(s), columns(h)], (1, 1))
                score = jnp.where(tile_mask(doc_ref, t, s), score, 0.0).astype(BF16)
                total += dot(score, value_ref[unit(s), columns(h)], (1, 0))
            out_ref[unit(t), columns(h)] = total


def attended_kernel(heads, doc_ref, query_ref, local_ref, cotangent_ref, gain_ref, prefix_ref,
                    out_ref, sums_ref, square, cross):
    tokens = query_ref.shape[0]
    offset = lax.axis_index("seq") * tokens
    step = pl.program_id(0)

    @pl.when(step == 0)
    def _():
        square[...] = jnp.zeros_like(square)
        cross[...] = jnp.zeros_like(cross)

    for u in range(tokens // UNIT):
        squares = square[unit(u), :]
        crosses = cross[unit(u), :]
        for h in range(heads):
            query = masked_rows(doc_ref[u * UNIT] < offset, query_ref[unit(u), columns(h)])
            prefix = prefix_ref[h * HEAD_DIM : (h + 1) * HEAD_DIM, :].astype(BF16)
            out = local_ref[unit(u), columns(h)] + dot(query, prefix, (1, 0))
            out_ref[unit(u), columns(h)] = out
            scaled = gain_ref[0:1, columns(h)] * cotangent_ref[unit(u), columns(h)].astype(F32)
            squares += out * out
            crosses += scaled * out
        square[unit(u), :] = squares
        cross[unit(u), :] = crosses

    @pl.when(step == pl.num_programs(0) - 1)
    def _():
        sums_ref[0:1, :] = jnp.sum(jnp.transpose(square[...]), axis=0, keepdims=True)
        sums_ref[1:2, :] = jnp.sum(jnp.transpose(cross[...]), axis=0, keepdims=True)


def norm_kernel(heads, features, doc_ref, sums_ref, out_ref, query_ref, cotangent_ref, gain_ref,
                normed_ref, grad_ref, state_ref, inverse, factor):
    tokens = query_ref.shape[0]
    offset = lax.axis_index("seq") * tokens

    @pl.when(pl.program_id(0) == 0)
    def _():
        sums = sums_ref[0] + sums_ref[1] + sums_ref[2] + sums_ref[3]
        inv = lax.rsqrt(sums[0:1] / features + epsilon)
        inverse[...] = column_of(inv)
        factor[...] = column_of(inv * inv * sums[1:2] / features)

    parts = HEAD_DIM // SLICE
    for h in range(heads):
        total = jnp.zeros((HEAD_DIM, HEAD_DIM), F32)
        for u in range(tokens // UNIT):
            out = out_ref[unit(u), columns(h)]
            gain = gain_ref[0:1, columns(h)]
            inv = inverse[unit(u), :]
            normed_ref[unit(u), columns(h)] = (out * inv * gain).astype(BF16)
            scaled = gain * cotangent_ref[unit(u), columns(h)].astype(F32)
            grad = (inv * (scaled - out * factor[unit(u), :])).astype(BF16)
            grad_ref[unit(u), columns(h)] = grad
            query = masked_rows(doc_ref[u * UNIT] < offset, query_ref[unit(u), columns(h)])
            total += dot(query, grad, (0, 0))
        state_ref[h * parts : (h + 1) * parts] = total.reshape(parts, SLICE, HEAD_DIM)


def back_kernel(heads, doc_ref, query_ref, key_ref, value_ref, grad_ref, prefix_ref,
                grad_q_ref, key_part_ref, value_part_ref):
    tokens = query_ref.shape[0]
    units = tokens // UNIT
    offset = lax.axis_index("seq") * tokens
    for h in range(heads):
        prefix = prefix_ref[h * HEAD_DIM : (h + 1) * HEAD_DIM, :].astype(BF16)
        grad_k = [jnp.zeros((UNIT, HEAD_DIM), F32) for _ in range(units)]
        grad_v = [jnp.zeros((UNIT, HEAD_DIM), F32) for _ in range(units)]
        for t in range(units):
            query = query_ref[unit(t), columns(h)]
            grad = grad_ref[unit(t), columns(h)]
            grad_q = dot(masked_rows(doc_ref[t * UNIT] < offset, grad), prefix, (1, 1))
            for s in range(t + 1):
                key = key_ref[unit(s), columns(h)]
                mask = tile_mask(doc_ref, t, s)
                score = jnp.where(mask, dot(query, key, (1, 1)), 0.0).astype(BF16)
                back = dot(grad, value_ref[unit(s), columns(h)], (1, 1))
                back = jnp.where(mask, back, 0.0).astype(BF16)
                grad_q += dot(back, key, (1, 0))
                grad_k[s] += dot(back, query, (0, 0))
                grad_v[s] += dot(score, grad, (0, 0))
            grad_q_ref[unit(t), columns(h)] = grad_q.astype(BF16)
        for s in range(units):
            key_part_ref[unit(s), columns(h)] = grad_k[s]
            value_part_ref[unit(s), columns(h)] = grad_v[s]


def finish_kernel(heads, doc_ref, key_ref, value_ref, key_part_ref, value_part_ref, suffix_ref,
                  grad_k_ref, grad_v_ref):
    tokens = key_ref.shape[0]
    last = doc_ref[tokens - 1]
    for h in range(heads):
        suffix = suffix_ref[h * HEAD_DIM : (h + 1) * HEAD_DIM, :].astype(BF16)
        for u in range(tokens // UNIT):
            closing = doc_ref[u * UNIT] == last
            value = masked_rows(closing, value_ref[unit(u), columns(h)])
            grad_k = key_part_ref[unit(u), columns(h)] + dot(value, suffix, (1, 1))
            grad_k_ref[unit(u), columns(h)] = grad_k.astype(BF16)
            key = masked_rows(closing, key_ref[unit(u), columns(h)])
            grad_v = value_part_ref[unit(u), columns(h)] + dot(key, suffix, (1, 0))
            grad_v_ref[unit(u), columns(h)] = grad_v.astype(BF16)


def on_device(queries, keys, values, cotangent, norm_gain, doc_start):
    tokens, width = queries.shape
    blocks = lax.axis_size("seq")
    heads = width // HEAD_DIM
    per_step = 2
    steps = heads // per_step
    parts = HEAD_DIM // SLICE
    features = width * lax.axis_size("head")
    gain = norm_gain.reshape(1, width)

    docs = pl.BlockSpec(memory_space=pltpu.SMEM)
    wide = pl.BlockSpec((tokens, per_step * HEAD_DIM), lambda i: (0, i))
    gains = pl.BlockSpec((1, per_step * HEAD_DIM), lambda i: (0, i))
    states = pl.BlockSpec((per_step * HEAD_DIM, HEAD_DIM), lambda i: (i, 0))
    tall = jax.ShapeDtypeStruct((tokens, width), F32)
    narrow = jax.ShapeDtypeStruct((tokens, width), BF16)

    def cost(products, arrays):
        return pl.CostEstimate(
            flops=2 * products * tokens * width, bytes_accessed=arrays * tokens * width, transcendentals=0
        )

    def call(kernel, ins, outs, shapes, estimate, scratch=()):
        return pl.pallas_call(
            kernel,
            grid=(steps,),
            in_specs=ins,
            out_specs=outs,
            out_shape=shapes,
            scratch_shapes=list(scratch),
            cost_estimate=estimate,
            compiler_params=pltpu.CompilerParams(vmem_limit_bytes=40 * 1024 * 1024),
        )

    tail = call(
        functools.partial(tail_kernel, per_step),
        [docs, wide, wide],
        pl.BlockSpec((per_step * parts, SLICE + 8, HEAD_DIM), lambda i: (i, 0, 0)),
        jax.ShapeDtypeStruct((blocks, SLICE + 8, HEAD_DIM), F32),
        cost(HEAD_DIM, 5),
    )(doc_start, keys, values)

    def exchange(data):
        return lax.all_to_all(data, "seq", 0, 0)

    def scan(part, flags, reverse):
        return pl.pallas_call(
            functools.partial(scan_kernel, reverse),
            out_shape=jax.ShapeDtypeStruct((blocks, SLICE, HEAD_DIM), F32),
        )(part, flags)

    tails = exchange(tail)
    flags = tails[:, SLICE:, :]
    prefix = exchange(scan(tails, flags, False)).reshape(heads * HEAD_DIM, HEAD_DIM)

    local = call(
        functools.partial(local_kernel, per_step),
        [docs, wide, wide, wide],
        wide,
        tall,
        cost(2 * 512, 10),
    )(doc_start, queries, keys, values)

    partial_rows = pltpu.VMEM((tokens, HEAD_DIM), F32)
    attended, sums = call(
        functools.partial(attended_kernel, per_step),
        [docs, wide, wide, wide, gains, states],
        [wide, pl.BlockSpec((2, tokens), lambda i: (0, 0))],
        [tall, jax.ShapeDtypeStruct((2, tokens), F32)],
        cost(HEAD_DIM, 12),
        [partial_rows, partial_rows],
    )(doc_start, queries, local, cotangent, gain, prefix)

    count = lax.axis_size("head")
    all_sums = jnp.stack(
        [sums]
        + [
            lax.ppermute(sums, "head", [(i, (i + step) % count) for i in range(count)])
            for step in range(1, count)
        ]
    )
    normed, grad_out, head_state = call(
        functools.partial(norm_kernel, per_step, features),
        [docs, pl.BlockSpec((count, 2, tokens), lambda i: (0, 0, 0)), wide, wide, wide, gains],
        [wide, wide, pl.BlockSpec((per_step * parts, SLICE, HEAD_DIM), lambda i: (i, 0, 0))],
        [narrow, narrow, jax.ShapeDtypeStruct((blocks, SLICE, HEAD_DIM), F32)],
        cost(HEAD_DIM, 13),
        [partial_rows, partial_rows],
    )(doc_start, all_sums, attended, queries, cotangent, gain)

    suffix = exchange(scan(exchange(head_state), flags, True)).reshape(heads * HEAD_DIM, HEAD_DIM)

    grad_q, key_part, value_part = call(
        functools.partial(back_kernel, per_step),
        [docs, wide, wide, wide, wide, states],
        [wide, wide, wide],
        [narrow, tall, tall],
        cost(5 * 512, 18),
    )(doc_start, queries, keys, values, grad_out, prefix)

    grad_k, grad_v = call(
        functools.partial(finish_kernel, per_step),
        [docs, wide, wide, wide, wide, states],
        [wide, wide],
        [narrow, narrow],
        cost(2 * HEAD_DIM, 16),
    )(doc_start, keys, values, key_part, value_part, suffix)
    return normed, grad_q, grad_k, grad_v


def solution(mesh):
    wide = P("seq", "head")
    return jax.shard_map(
        on_device,
        mesh=mesh,
        in_specs=(wide, wide, wide, wide, P("head"), P("seq")),
        out_specs=(wide, wide, wide, wide),
        check_vma=False,
    )
```

```python
import functools

import jax
import jax.numpy as jnp
from jax import lax
from jax.experimental import pallas as pl
from jax.experimental.pallas import tpu as pltpu
from jax.sharding import PartitionSpec as P

HEAD_DIM = 128
UNIT = 256
SLICE = 16
VMEM = 58 * 1024 * 1024
SMALL_VMEM = 8 * 1024 * 1024
epsilon = 1e-06

F32 = jnp.float32
BF16 = jnp.bfloat16


def dot(left, right, contract):
    return lax.dot_general(
        left, right, ((contract[0:1], contract[1:2]), ((), ())), preferred_element_type=F32
    )


def unit(index):
    return slice(index * UNIT, (index + 1) * UNIT)


def columns(index):
    return slice(index * HEAD_DIM, (index + 1) * HEAD_DIM)


def causal():
    rows = lax.broadcasted_iota(jnp.int32, (UNIT, UNIT), 0)
    return rows >= lax.broadcasted_iota(jnp.int32, (UNIT, UNIT), 1)


def tile_mask(doc_ref, later, earlier):
    if later == earlier:
        return causal()
    return jnp.full((UNIT, UNIT), doc_ref[later * UNIT] == doc_ref[earlier * UNIT])


def masked_rows(keep, rows):
    return jnp.where(jnp.full(rows.shape, keep), rows, jnp.zeros_like(rows))


def column_of(row):
    return jnp.transpose(jnp.broadcast_to(row, (HEAD_DIM, row.shape[1])))


def tail_kernel(heads, doc_ref, place_ref, key_ref, value_ref, theirs_ref, mine_ref):
    tokens = key_ref.shape[0]
    last = doc_ref[tokens - 1]
    step = pl.program_id(0)
    half = pl.num_programs(0) // 2
    size = heads * HEAD_DIM // SLICE
    flag = jnp.where(last >= place_ref[0], 0.0, 1.0).astype(F32)
    states = []
    for h in range(heads):
        total = jnp.zeros((HEAD_DIM, HEAD_DIM), F32)
        for u in range(tokens // UNIT):
            key = masked_rows(doc_ref[u * UNIT] == last, key_ref[unit(u), columns(h)])
            total += dot(key, value_ref[unit(u), columns(h)], (0, 0))
        states.append(total)
    parts = jnp.concatenate(states, 0).reshape(size, SLICE, HEAD_DIM)

    @pl.when(step < half)
    def _():
        theirs_ref[pl.ds(step * size, size)] = parts
        theirs_ref[half * size] = jnp.full((SLICE, HEAD_DIM), flag)

    @pl.when(step >= half)
    def _():
        mine_ref[pl.ds((step - half) * size, size)] = parts
        mine_ref[half * size] = jnp.full((SLICE, HEAD_DIM), flag)


def combine_kernel(first_core, place_ref, mine_ref, theirs_ref, total_ref):
    rows = total_ref.shape[0]
    my_flag, their_flag = mine_ref[rows, 0:1, :], theirs_ref[rows, 0:1, :]
    first = jnp.full((SLICE, HEAD_DIM), place_ref[1] == first_core)
    for i in range(rows):
        mine, theirs = mine_ref[i], theirs_ref[i]
        total_ref[i, 0:SLICE, :] = jnp.where(
            first, theirs + their_flag * mine, mine + my_flag * theirs
        )
    if total_ref.shape[1] > SLICE:
        total_ref[:, SLICE:, :] = jnp.broadcast_to(my_flag * their_flag, (rows, 8, HEAD_DIM))


def spread_kernel(first_core, place_ref, entering_ref, mine_ref, theirs_ref, own_ref, other_ref):
    rows = entering_ref.shape[0]
    my_flag, their_flag = mine_ref[rows, 0:1, :], theirs_ref[rows, 0:1, :]
    first = jnp.full((SLICE, HEAD_DIM), place_ref[1] == first_core)
    for i in range(rows):
        entering = entering_ref[i]
        place = slice(i * SLICE, (i + 1) * SLICE)
        own_ref[place, :] = jnp.where(first, entering, theirs_ref[i] + their_flag * entering)
        other_ref[place, :] = jnp.where(first, mine_ref[i] + my_flag * entering, entering)


def scan_kernel(reverse, part_ref, flag_ref, state_ref):
    count = part_ref.shape[0]
    carry = jnp.zeros((SLICE, HEAD_DIM), F32)
    for step in range(count):
        b = count - 1 - step if reverse else step
        state_ref[b] = carry
        carry = part_ref[b, 0:SLICE, :] + flag_ref[b, SLICE : SLICE + 1, :] * carry


def pick(place_ref, mine_ref, theirs_ref, h):
    is_mine = pl.program_id(0) // (pl.num_programs(0) // 2) == place_ref[1]
    rows = slice(h * HEAD_DIM, (h + 1) * HEAD_DIM)
    keep = jnp.full((HEAD_DIM, HEAD_DIM), is_mine)
    return jnp.where(keep, mine_ref[rows, :], theirs_ref[rows, :]).astype(BF16)


def attended_kernel(heads, doc_ref, place_ref, query_ref, local_ref, cotangent_ref, gain_ref,
                    mine_ref, theirs_ref, out_ref, sums_ref, square, cross):
    tokens = query_ref.shape[0]
    offset = place_ref[0]
    step = pl.program_id(0)

    @pl.when(step == 0)
    def _():
        square[...] = jnp.zeros_like(square)
        cross[...] = jnp.zeros_like(cross)

    for u in range(tokens // UNIT):
        squares = square[unit(u), :]
        crosses = cross[unit(u), :]
        for h in range(heads):
            query = masked_rows(doc_ref[u * UNIT] < offset, query_ref[unit(u), columns(h)])
            prefix = pick(place_ref, mine_ref, theirs_ref, h)
            out = local_ref[unit(u), columns(h)] + dot(query, prefix, (1, 0))
            out_ref[unit(u), columns(h)] = out
            scaled = gain_ref[0:1, columns(h)] * cotangent_ref[unit(u), columns(h)].astype(F32)
            squares += out * out
            crosses += scaled * out
        square[unit(u), :] = squares
        cross[unit(u), :] = crosses

    @pl.when(step == pl.num_programs(0) - 1)
    def _():
        sums_ref[0:1, :] = jnp.sum(jnp.transpose(square[...]), axis=0, keepdims=True)
        sums_ref[1:2, :] = jnp.sum(jnp.transpose(cross[...]), axis=0, keepdims=True)


def norm_kernel(heads, features, doc_ref, place_ref, sums_ref, sums1_ref, sums2_ref, sums3_ref,
                out_ref, query_ref, cotangent_ref, gain_ref, normed_ref, grad_ref, theirs_ref, mine_ref, inverse, factor):
    tokens = query_ref.shape[0]
    step = pl.program_id(0)
    half = pl.num_programs(0) // 2
    size = heads * HEAD_DIM // SLICE
    flag = jnp.where(doc_ref[tokens - 1] >= place_ref[0], 0.0, 1.0).astype(F32)

    @pl.when(step == 0)
    def _():
        sums = sums_ref[...] + sums1_ref[...] + sums2_ref[...] + sums3_ref[...]
        inv = lax.rsqrt(sums[0:1] / features + epsilon)
        inverse[...] = column_of(inv)
        factor[...] = column_of(inv * inv * sums[1:2] / features)

    states = []
    for h in range(heads):
        total = jnp.zeros((HEAD_DIM, HEAD_DIM), F32)
        for u in range(tokens // UNIT):
            out = out_ref[unit(u), columns(h)]
            gain = gain_ref[0:1, columns(h)]
            inv = inverse[unit(u), :]
            normed_ref[unit(u), columns(h)] = (out * inv * gain).astype(BF16)
            scaled = gain * cotangent_ref[unit(u), columns(h)].astype(F32)
            grad = (inv * (scaled - out * factor[unit(u), :])).astype(BF16)
            grad_ref[unit(u), columns(h)] = grad
            query = masked_rows(doc_ref[u * UNIT] < place_ref[0], query_ref[unit(u), columns(h)])
            total += dot(query, grad, (0, 0))
        states.append(total)
    parts = jnp.concatenate(states, 0).reshape(size, SLICE, HEAD_DIM)

    @pl.when(step < half)
    def _():
        theirs_ref[pl.ds(step * size, size)] = parts
        theirs_ref[half * size] = jnp.full((SLICE, HEAD_DIM), flag)

    @pl.when(step >= half)
    def _():
        mine_ref[pl.ds((step - half) * size, size)] = parts
        mine_ref[half * size] = jnp.full((SLICE, HEAD_DIM), flag)


def rows_from(unit_index):
    return slice(unit_index * UNIT, None)


def lower_scores(doc_ref, left_ref, right_ref, s, h):
    scores = dot(left_ref[rows_from(s), columns(h)], right_ref[unit(s), columns(h)], (1, 1))
    units = left_ref.shape[0] // UNIT
    tiles = [
        jnp.where(tile_mask(doc_ref, t, s), scores[unit(t - s)], 0.0).astype(BF16)
        for t in range(s, units)
    ]
    return jnp.concatenate(tiles, 0)


def local_kernel(heads, doc_ref, query_ref, key_ref, value_ref, out_ref):
    for h in range(heads):
        for s in range(query_ref.shape[0] // UNIT):
            attend = lower_scores(doc_ref, query_ref, key_ref, s, h)
            part = dot(attend, value_ref[unit(s), columns(h)], (1, 0))
            if s == 0:
                out_ref[:, columns(h)] = part
            else:
                out_ref[rows_from(s), columns(h)] += part


def back_kernel(heads, doc_ref, place_ref, query_ref, key_ref, value_ref, grad_ref, mine_ref,
                theirs_ref, grad_q_ref, key_part_ref, grad_q):
    units = query_ref.shape[0] // UNIT
    for h in range(heads):
        prefix = pick(place_ref, mine_ref, theirs_ref, h)
        for t in range(units):
            carried = masked_rows(doc_ref[t * UNIT] < place_ref[0], grad_ref[unit(t), columns(h)])
            grad_q[unit(t), columns(h)] = dot(carried, prefix, (1, 1))
        for s in range(units):
            backs = lower_scores(doc_ref, grad_ref, value_ref, s, h)
            grad_q[rows_from(s), columns(h)] += dot(backs, key_ref[unit(s), columns(h)], (1, 0))
            key_part_ref[unit(s), columns(h)] = dot(
                backs, query_ref[rows_from(s), columns(h)], (0, 0)
            )
        grad_q_ref[:, columns(h)] = grad_q[:, columns(h)].astype(BF16)


def value_kernel(heads, doc_ref, query_ref, key_ref, grad_ref, value_part_ref):
    for h in range(heads):
        for s in range(query_ref.shape[0] // UNIT):
            attend = lower_scores(doc_ref, query_ref, key_ref, s, h)
            value_part_ref[unit(s), columns(h)] = dot(
                attend, grad_ref[rows_from(s), columns(h)], (0, 0)
            )


def finish_kernel(heads, doc_ref, place_ref, key_ref, value_ref, key_part_ref, value_part_ref,
                  mine_ref, theirs_ref, grad_k_ref, grad_v_ref):
    tokens = key_ref.shape[0]
    last = doc_ref[tokens - 1]
    for h in range(heads):
        suffix = pick(place_ref, mine_ref, theirs_ref, h)
        for u in range(tokens // UNIT):
            closing = doc_ref[u * UNIT] == last
            value = masked_rows(closing, value_ref[unit(u), columns(h)])
            grad_k = key_part_ref[unit(u), columns(h)] + dot(value, suffix, (1, 1))
            grad_k_ref[unit(u), columns(h)] = grad_k.astype(BF16)
            key = masked_rows(closing, key_ref[unit(u), columns(h)])
            grad_v = value_part_ref[unit(u), columns(h)] + dot(key, suffix, (1, 0))
            grad_v_ref[unit(u), columns(h)] = grad_v.astype(BF16)


def on_device(queries, keys, values, cotangent, norm_gain, doc_start):
    tokens, width = queries.shape
    blocks = lax.axis_size("seq")
    chips = blocks // 2
    heads = width // HEAD_DIM
    per_step = 2
    steps = heads // per_step
    features = width * lax.axis_size("head")
    gain = norm_gain.reshape(1, width)
    block = lax.axis_index("seq")
    core = block % 2
    place = jnp.stack([block * tokens, core]).astype(jnp.int32)

    def straight(i, place_ref):
        return i

    def theirs_first(i, place_ref):
        return per_step * ((i // 2) ^ (1 - place_ref[1])) + i % 2

    step_cols = per_step * HEAD_DIM
    docs = pl.BlockSpec(memory_space=pltpu.SMEM)

    def wide(order):
        return pl.BlockSpec((tokens, step_cols), lambda i, p: (0, order(i, p)))

    def gains(order):
        return pl.BlockSpec((1, step_cols), lambda i, p: (0, order(i, p)))

    def whole(*shape):
        return pl.BlockSpec(shape, lambda i, p: (0,) * len(shape))

    halves = pl.BlockSpec((step_cols, HEAD_DIM), lambda i, p: (i % 2, 0))
    tall = jax.ShapeDtypeStruct((tokens, width), F32)
    narrow = jax.ShapeDtypeStruct((tokens, width), BF16)

    def state(*shape):
        return jax.ShapeDtypeStruct(shape, F32)

    def call(kernel, ins, outs, shapes, products, arrays, scratch=()):
        def body(place_ref, doc_ref, *refs):
            kernel(doc_ref, place_ref, *refs)

        return functools.partial(
            pl.pallas_call(
                body,
                grid_spec=pltpu.PrefetchScalarGridSpec(
                    num_scalar_prefetch=1,
                    grid=(steps,),
                    in_specs=[docs] + ins,
                    out_specs=outs,
                    scratch_shapes=list(scratch),
                ),
                out_shape=shapes,
                cost_estimate=pl.CostEstimate(
                    flops=2 * products * tokens * width,
                    bytes_accessed=arrays * tokens * width,
                    transcendentals=0,
                ),
                compiler_params=pltpu.CompilerParams(vmem_limit_bytes=VMEM),
            ),
            place,
            doc_start,
        )

    def placeless(kernel):
        return lambda doc_ref, place_ref, *refs: kernel(doc_ref, *refs)

    rows = heads // 2 * HEAD_DIM // SLICE
    theirs, mine = call(
        functools.partial(tail_kernel, per_step),
        [wide(theirs_first), wide(theirs_first)],
        [whole(rows + 1, SLICE, HEAD_DIM)] * 2,
        [state(rows + 1, SLICE, HEAD_DIM)] * 2,
        HEAD_DIM,
        5,
    )(keys, values)

    def sibling(data):
        return lax.ppermute(data, "seq", [(i, i ^ 1) for i in range(blocks)])

    groups = [[2 * chip + c for chip in range(chips)] for c in range(2)]

    def exchange(data):
        return lax.all_to_all(data, "seq", 0, 0, axis_index_groups=groups)

    def small(kernel, shapes, *operands):
        return pl.pallas_call(
            kernel,
            in_specs=[
                pl.BlockSpec(memory_space=pltpu.SMEM if operand is place else pltpu.VMEM)
                for operand in operands
            ],
            out_shape=shapes,
            compiler_params=pltpu.CompilerParams(vmem_limit_bytes=SMALL_VMEM),
        )(*operands)

    def scan(part, flags, reverse):
        kernel = functools.partial(scan_kernel, reverse)
        return small(kernel, state(rows, SLICE, HEAD_DIM), part, flags)

    def combine(first_core, mine, received, depth):
        kernel = functools.partial(combine_kernel, first_core)
        return small(kernel, state(rows, depth, HEAD_DIM), place, mine, received)

    def spread(first_core, entering, mine, received):
        kernel = functools.partial(spread_kernel, first_core)
        shape = state(rows * SLICE, HEAD_DIM)
        own, other = small(kernel, [shape, shape], place, entering, mine, received)
        return own, sibling(other)

    received = sibling(theirs)
    flags = exchange(combine(0, mine, received, SLICE + 8))
    entering = exchange(scan(flags, flags, False))
    local = call(
        placeless(functools.partial(local_kernel, per_step)),
        [wide(straight)] * 3,
        wide(straight),
        tall,
        2 * 512,
        10,
    )(queries, keys, values)

    entering, local = lax.optimization_barrier((entering, local))
    prefix = spread(0, entering, mine, received)

    partial_rows = pltpu.VMEM((tokens, HEAD_DIM), F32)
    attended, sums = call(
        functools.partial(attended_kernel, per_step),
        [wide(straight)] * 3 + [gains(straight), halves, halves],
        [wide(straight), whole(2, tokens)],
        [tall, state(2, tokens)],
        HEAD_DIM,
        12,
        [partial_rows, partial_rows],
    )(queries, local, cotangent, gain, *prefix)

    count = lax.axis_size("head")
    all_sums = [sums] + [
        lax.ppermute(sums, "head", [(i, (i + step) % count) for i in range(count)])
        for step in range(1, count)
    ]
    normed, grad_out, theirs, mine = call(
        functools.partial(norm_kernel, per_step, features),
        [whole(2, tokens)] * count + [wide(theirs_first)] * 3 + [gains(theirs_first)],
        [wide(theirs_first)] * 2 + [whole(rows + 1, SLICE, HEAD_DIM)] * 2,
        [narrow, narrow] + [state(rows + 1, SLICE, HEAD_DIM)] * 2,
        HEAD_DIM,
        13,
        [partial_rows, partial_rows],
    )(*all_sums, attended, queries, cotangent, gain)

    received = sibling(theirs)
    gathered = exchange(combine(1, mine, received, SLICE))
    grad_q, key_part = call(
        functools.partial(back_kernel, per_step),
        [wide(straight)] * 4 + [halves, halves],
        [wide(straight)] * 2,
        [narrow, tall],
        3 * 512 + HEAD_DIM,
        14,
        [pltpu.VMEM((tokens, step_cols), F32)],
    )(queries, keys, values, grad_out, *prefix)
    gathered, grad_q, key_part = lax.optimization_barrier((gathered, grad_q, key_part))
    entering = exchange(scan(gathered, flags, True))
    value_part = call(
        placeless(functools.partial(value_kernel, per_step)),
        [wide(straight)] * 3,
        wide(straight),
        tall,
        2 * 512,
        10,
    )(queries, keys, grad_out)
    entering, value_part = lax.optimization_barrier((entering, value_part))
    suffix = spread(1, entering, mine, received)

    grad_k, grad_v = call(
        functools.partial(finish_kernel, per_step),
        [wide(straight)] * 4 + [halves, halves],
        [wide(straight)] * 2,
        [narrow, narrow],
        2 * HEAD_DIM,
        16,
    )(keys, values, key_part, value_part, *suffix)
    return normed, grad_q, grad_k, grad_v


def solution(mesh):
    wide = P("seq", "head")
    return jax.shard_map(
        on_device,
        mesh=mesh,
        in_specs=(wide, wide, wide, wide, P("head"), P("seq")),
        out_specs=(wide, wide, wide, wide),
        check_vma=False,
    )
```

```python
import functools

import jax
import jax.numpy as jnp
from jax import lax
from jax.experimental import pallas as pl
from jax.experimental.pallas import tpu as pltpu
from jax.sharding import PartitionSpec as P

HEAD_DIM = 128
UNIT = 256
SLICE = 16
ROWS = 256
VMEM = 58 * 1024 * 1024
ROW_VMEM = 58 * 1024 * 1024
SMALL_VMEM = 8 * 1024 * 1024
epsilon = 1e-06

F32 = jnp.float32
BF16 = jnp.bfloat16


def dot(left, right, contract):
    return lax.dot_general(
        left, right, ((contract[0:1], contract[1:2]), ((), ())), preferred_element_type=F32
    )


def unit(index):
    return slice(index * UNIT, (index + 1) * UNIT)


def columns(index):
    return slice(index * HEAD_DIM, (index + 1) * HEAD_DIM)


def causal(later_dim=0):
    later = lax.broadcasted_iota(jnp.int32, (UNIT, UNIT), later_dim)
    return later >= lax.broadcasted_iota(jnp.int32, (UNIT, UNIT), 1 - later_dim)


def tile_mask(doc_ref, later, earlier):
    if later == earlier:
        return causal()
    return jnp.full((UNIT, UNIT), doc_ref[later * UNIT] == doc_ref[earlier * UNIT])


def masked_rows(keep, rows):
    return jnp.where(jnp.full(rows.shape, keep), rows, jnp.zeros_like(rows))


def column_of(row):
    return jnp.transpose(jnp.broadcast_to(row, (HEAD_DIM, row.shape[1])))


def add_state(total, left_ref, right_ref, keep, heads):
    for h in range(heads):
        left = masked_rows(keep, left_ref[:, columns(h)])
        total[columns(h), :] += dot(left, right_ref[:, columns(h)], (0, 0))


def split_state(total, doc_ref, place_ref, theirs_ref, mine_ref):
    rows = total.shape[0] // (2 * SLICE)
    flag = jnp.where(doc_ref[doc_ref.shape[0] - 1] >= place_ref[0], 0.0, 1.0).astype(F32)
    low = total[: rows * SLICE, :].reshape(rows, SLICE, HEAD_DIM)
    high = total[rows * SLICE :, :].reshape(rows, SLICE, HEAD_DIM)
    is_low = jnp.full(low.shape, place_ref[1] == 0)
    mine_ref[0:rows] = jnp.where(is_low, low, high)
    theirs_ref[0:rows] = jnp.where(is_low, high, low)
    mine_ref[rows] = jnp.full((SLICE, HEAD_DIM), flag)
    theirs_ref[rows] = jnp.full((SLICE, HEAD_DIM), flag)


def streamed(kernel, before, after, ins, outs):
    def body(doc_ref, place_ref, *refs):
        sources, rest = refs[:ins], refs[ins:]
        targets, rest = rest[-outs:] if outs else (), rest[: len(rest) - outs] if outs else rest
        buffers, sems = rest[-1 - ins - outs : -1], rest[-1]
        rest = rest[: -1 - ins - outs]
        bands = doc_ref.shape[0] // ROWS

        def copy(k, i):
            rows = pl.ds(i * ROWS, ROWS)
            if k < ins:
                ends = sources[k].at[rows], buffers[k].at[rows]
            else:
                ends = buffers[k].at[rows], targets[k - ins].at[rows]
            return pltpu.make_async_copy(*ends, sems.at[k, i])

        for i in range(bands):
            for k in range(ins):
                copy(k, i).start()
        if before is not None:
            before(doc_ref, place_ref, *rest)
        for i in range(bands):
            for k in range(ins):
                copy(k, i).wait()
            views = [b.at[pl.ds(i * ROWS, ROWS)] for b in buffers]
            kernel(i, doc_ref, place_ref, *views, *rest)
            for k in range(ins, ins + outs):
                copy(k, i).start()
        if after is not None:
            after(doc_ref, place_ref, *rest)
        for i in range(bands):
            for k in range(ins, ins + outs):
                copy(k, i).wait()

    return body


def add_state(total, left_ref, right_ref, keep, heads):
    for h in range(heads):
        left = masked_rows(keep, left_ref[:, columns(h)])
        total[columns(h), :] += dot(left, right_ref[:, columns(h)], (0, 0))


def split_state(doc_ref, place_ref, *refs):
    theirs_ref, mine_ref, total = refs[-3:]
    rows = total.shape[0] // (2 * SLICE)
    flag = jnp.where(doc_ref[doc_ref.shape[0] - 1] >= place_ref[0], 0.0, 1.0).astype(F32)
    low = total[: rows * SLICE, :].reshape(rows, SLICE, HEAD_DIM)
    high = total[rows * SLICE :, :].reshape(rows, SLICE, HEAD_DIM)
    is_low = jnp.full(low.shape, place_ref[1] == 0)
    mine_ref[0:rows] = jnp.where(is_low, low, high)
    theirs_ref[0:rows] = jnp.where(is_low, high, low)
    mine_ref[rows] = jnp.full((SLICE, HEAD_DIM), flag)
    theirs_ref[rows] = jnp.full((SLICE, HEAD_DIM), flag)


def clear_state(doc_ref, place_ref, *refs):
    refs[-1][...] = jnp.zeros_like(refs[-1])


def tail_kernel(heads, i, doc_ref, place_ref, key_ref, value_ref, theirs_ref, mine_ref, total):
    keep = doc_ref[i * ROWS] == doc_ref[doc_ref.shape[0] - 1]
    add_state(total, key_ref, value_ref, keep, heads)


def combine_kernel(first_core, place_ref, mine_ref, theirs_ref, total_ref):
    rows = total_ref.shape[0]
    my_flag, their_flag = mine_ref[rows, 0:1, :], theirs_ref[rows, 0:1, :]
    first = jnp.full((SLICE, HEAD_DIM), place_ref[1] == first_core)
    for i in range(rows):
        mine, theirs = mine_ref[i], theirs_ref[i]
        total_ref[i, 0:SLICE, :] = jnp.where(
            first, theirs + their_flag * mine, mine + my_flag * theirs
        )
    if total_ref.shape[1] > SLICE:
        total_ref[:, SLICE:, :] = jnp.broadcast_to(my_flag * their_flag, (rows, 8, HEAD_DIM))


def spread_kernel(first_core, place_ref, entering_ref, mine_ref, theirs_ref, own_ref, other_ref):
    rows = entering_ref.shape[0]
    my_flag, their_flag = mine_ref[rows, 0:1, :], theirs_ref[rows, 0:1, :]
    first = jnp.full((SLICE, HEAD_DIM), place_ref[1] == first_core)
    for i in range(rows):
        entering = entering_ref[i]
        place = slice(i * SLICE, (i + 1) * SLICE)
        own_ref[place, :] = jnp.where(first, entering, theirs_ref[i] + their_flag * entering)
        other_ref[place, :] = jnp.where(first, mine_ref[i] + my_flag * entering, entering)


def scan_kernel(reverse, part_ref, flag_ref, state_ref):
    count = part_ref.shape[0]
    carry = jnp.zeros((SLICE, HEAD_DIM), F32)
    for step in range(count):
        b = count - 1 - step if reverse else step
        state_ref[b] = carry
        carry = part_ref[b, 0:SLICE, :] + flag_ref[b, SLICE : SLICE + 1, :] * carry


def picked(place_ref, mine_ref, theirs_ref, is_mine, h):
    rows = slice(h * HEAD_DIM, (h + 1) * HEAD_DIM)
    keep = jnp.full((HEAD_DIM, HEAD_DIM), is_mine)
    return jnp.where(keep, mine_ref[rows, :], theirs_ref[rows, :]).astype(BF16)


def pick(place_ref, mine_ref, theirs_ref, h):
    is_mine = pl.program_id(0) // (pl.num_programs(0) // 2) == place_ref[1]
    return picked(place_ref, mine_ref, theirs_ref, is_mine, h)


def pick_head(place_ref, mine_ref, theirs_ref, heads, h):
    half = heads // 2
    return picked(place_ref, mine_ref, theirs_ref, place_ref[1] == h // half, h % half)


def attended_kernel(heads, i, doc_ref, place_ref, query_ref, local_ref, cotangent_ref, out_ref,
                    gain_ref, mine_ref, theirs_ref, sums_ref):
    carried = doc_ref[i * ROWS] < place_ref[0]
    squares = jnp.zeros((ROWS, HEAD_DIM), F32)
    crosses = jnp.zeros((ROWS, HEAD_DIM), F32)
    for h in range(heads):
        query = masked_rows(carried, query_ref[:, columns(h)])
        prefix = pick_head(place_ref, mine_ref, theirs_ref, heads, h)
        out = local_ref[:, columns(h)] + dot(query, prefix, (1, 0))
        out_ref[:, columns(h)] = out
        scaled = gain_ref[0:1, columns(h)] * cotangent_ref[:, columns(h)].astype(F32)
        squares += out * out
        crosses += scaled * out
    band = slice(i * ROWS, (i + 1) * ROWS)
    sums_ref[0:1, band] = jnp.sum(jnp.transpose(squares), axis=0, keepdims=True)
    sums_ref[1:2, band] = jnp.sum(jnp.transpose(crosses), axis=0, keepdims=True)


def norm_kernel(heads, features, i, doc_ref, place_ref, out_ref, query_ref, cotangent_ref,
                normed_ref, grad_ref, gain_ref, sums_ref, sums1_ref, sums2_ref, sums3_ref,
                theirs_ref, mine_ref, total):
    band = slice(i * ROWS, (i + 1) * ROWS)
    sums = sums_ref[:, band] + sums1_ref[:, band] + sums2_ref[:, band] + sums3_ref[:, band]
    inv_row = lax.rsqrt(sums[0:1] / features + epsilon)
    inv = column_of(inv_row)
    factor = column_of(inv_row * inv_row * sums[1:2] / features)
    for h in range(heads):
        out = out_ref[:, columns(h)]
        gain = gain_ref[0:1, columns(h)]
        normed_ref[:, columns(h)] = (out * inv * gain).astype(BF16)
        scaled = gain * cotangent_ref[:, columns(h)].astype(F32)
        grad_ref[:, columns(h)] = (inv * (scaled - out * factor)).astype(BF16)
    add_state(total, query_ref, grad_ref, doc_ref[i * ROWS] < place_ref[0], heads)


def rows_from(unit_index):
    return slice(unit_index * UNIT, None)


def lower_scores(doc_ref, left_ref, right_ref, s, h):
    scores = dot(left_ref[rows_from(s), columns(h)], right_ref[unit(s), columns(h)], (1, 1))
    units = left_ref.shape[0] // UNIT
    tiles = [
        jnp.where(tile_mask(doc_ref, t, s), scores[unit(t - s)], 0.0).astype(BF16)
        for t in range(s, units)
    ]
    return jnp.concatenate(tiles, 0)


def upper_scores(doc_ref, left_ref, right_ref, s, h):
    scores = dot(left_ref[unit(s), columns(h)], right_ref[rows_from(s), columns(h)], (1, 1))
    tiles = []
    for t in range(s, right_ref.shape[0] // UNIT):
        mask = tile_mask(doc_ref, t, s) if t > s else causal(1)
        tiles.append(jnp.where(mask, scores[:, unit(t - s)], 0.0).astype(BF16))
    return jnp.concatenate(tiles, 1)


def local_kernel(heads, doc_ref, query_ref, key_ref, value_ref, out_ref):
    for h in range(heads):
        for s in range(query_ref.shape[0] // UNIT):
            attend = lower_scores(doc_ref, query_ref, key_ref, s, h)
            part = dot(attend, value_ref[unit(s), columns(h)], (1, 0))
            if s == 0:
                out_ref[:, columns(h)] = part
            else:
                out_ref[rows_from(s), columns(h)] += part


def back_kernel(heads, doc_ref, place_ref, query_ref, key_ref, value_ref, grad_ref, mine_ref,
                theirs_ref, grad_q_ref, key_part_ref, grad_q):
    units = query_ref.shape[0] // UNIT
    for h in range(heads):
        prefix = pick(place_ref, mine_ref, theirs_ref, h)
        for t in range(units):
            carried = masked_rows(doc_ref[t * UNIT] < place_ref[0], grad_ref[unit(t), columns(h)])
            grad_q[unit(t), columns(h)] = dot(carried, prefix, (1, 1))
        for s in range(units):
            backs = lower_scores(doc_ref, grad_ref, value_ref, s, h)
            grad_q[rows_from(s), columns(h)] += dot(backs, key_ref[unit(s), columns(h)], (1, 0))
            key_part_ref[unit(s), columns(h)] = dot(
                backs, query_ref[rows_from(s), columns(h)], (0, 0)
            )
        grad_q_ref[:, columns(h)] = grad_q[:, columns(h)].astype(BF16)


def value_kernel(heads, doc_ref, query_ref, key_ref, grad_ref, value_part_ref):
    for h in range(heads):
        for s in range(query_ref.shape[0] // UNIT):
            attend = upper_scores(doc_ref, key_ref, query_ref, s, h)
            value_part_ref[unit(s), columns(h)] = dot(
                attend, grad_ref[rows_from(s), columns(h)], (1, 0)
            )


def finish_kernel(heads, i, doc_ref, place_ref, key_ref, value_ref, key_part_ref,
                  value_part_ref, grad_k_ref, grad_v_ref, mine_ref, theirs_ref):
    closing = doc_ref[i * ROWS] == doc_ref[doc_ref.shape[0] - 1]
    for h in range(heads):
        suffix = pick_head(place_ref, mine_ref, theirs_ref, heads, h)
        value = masked_rows(closing, value_ref[:, columns(h)])
        grad_k = key_part_ref[:, columns(h)] + dot(value, suffix, (1, 1))
        grad_k_ref[:, columns(h)] = grad_k.astype(BF16)
        key = masked_rows(closing, key_ref[:, columns(h)])
        grad_v = value_part_ref[:, columns(h)] + dot(key, suffix, (1, 0))
        grad_v_ref[:, columns(h)] = grad_v.astype(BF16)


def on_device(queries, keys, values, cotangent, norm_gain, doc_start):
    tokens, width = queries.shape
    blocks = lax.axis_size("seq")
    chips = blocks // 2
    heads = width // HEAD_DIM
    per_step = 2
    steps = heads // per_step
    features = width * lax.axis_size("head")
    gain = norm_gain.reshape(1, width)

    def here():
        block = lax.axis_index("seq")
        return block * tokens, lax.rem(block, 2)

    step_cols = per_step * HEAD_DIM
    docs = pl.BlockSpec(memory_space=pltpu.SMEM)

    wide = pl.BlockSpec((tokens, step_cols), lambda i: (0, i))
    anywhere = pl.BlockSpec(memory_space=pl.ANY)
    vmem = pl.BlockSpec(memory_space=pltpu.VMEM)

    def stream(kernel, arrays, operands, wide_outs, outs, products, traffic, before=None,
               after=None, scratch=()):
        ins, count = len(arrays), len(wide_outs)
        inner = streamed(kernel, before, after, ins, count)

        def body(doc_ref, *refs):
            front, rest = refs[: ins + len(operands)], refs[ins + len(operands) :]
            big, small_outs = rest[:count], rest[count : count + len(outs)]
            extra = rest[count + len(outs) :]
            own, buffers = extra[: len(scratch)], extra[len(scratch) :]
            inner(doc_ref, here(), *front, *small_outs, *own, *buffers, *big)

        return pl.pallas_call(
            body,
            in_specs=[docs] + [anywhere] * ins + [vmem] * len(operands),
            out_specs=[anywhere] * count + [vmem] * len(outs),
            out_shape=list(wide_outs) + list(outs),
            scratch_shapes=list(scratch)
            + [pltpu.VMEM(a.shape, a.dtype) for a in list(arrays) + list(wide_outs)]
            + [pltpu.SemaphoreType.DMA((ins + count, tokens // ROWS))],
            cost_estimate=pl.CostEstimate(
                flops=2 * products * tokens * width,
                bytes_accessed=traffic * tokens * width,
                transcendentals=0,
            ),
            compiler_params=pltpu.CompilerParams(vmem_limit_bytes=ROW_VMEM),
        )(doc_start, *arrays, *operands)

    halves = pl.BlockSpec((step_cols, HEAD_DIM), lambda i: (i % 2, 0))
    tall = jax.ShapeDtypeStruct((tokens, width), F32)
    narrow = jax.ShapeDtypeStruct((tokens, width), BF16)

    def state(*shape):
        return jax.ShapeDtypeStruct(shape, F32)

    def call(kernel, ins, outs, shapes, products, arrays, scratch=()):
        def body(doc_ref, *refs):
            kernel(doc_ref, here(), *refs)

        return functools.partial(
            pl.pallas_call(
                body,
                grid=(steps,),
                in_specs=[docs] + ins,
                out_specs=outs,
                scratch_shapes=list(scratch),
                out_shape=shapes,
                cost_estimate=pl.CostEstimate(
                    flops=2 * products * tokens * width,
                    bytes_accessed=arrays * tokens * width,
                    transcendentals=0,
                ),
                compiler_params=pltpu.CompilerParams(vmem_limit_bytes=VMEM),
            ),
            doc_start,
        )

    def placeless(kernel):
        return lambda doc_ref, place_ref, *refs: kernel(doc_ref, *refs)

    rows = heads // 2 * HEAD_DIM // SLICE
    total_rows = pltpu.VMEM((width, HEAD_DIM), F32)
    parted = [state(rows + 1, SLICE, HEAD_DIM)] * 2
    theirs, mine = stream(
        functools.partial(tail_kernel, heads),
        [keys, values], [], [], parted, HEAD_DIM, 5, clear_state, split_state, [total_rows],
    )

    def sibling(data):
        return lax.ppermute(data, "seq", [(i, i ^ 1) for i in range(blocks)])

    groups = [[2 * chip + c for chip in range(chips)] for c in range(2)]

    def exchange(data):
        return lax.all_to_all(data, "seq", 0, 0, axis_index_groups=groups)

    def small(kernel, shapes, *operands):
        return pl.pallas_call(
            kernel,
            out_shape=shapes,
            compiler_params=pltpu.CompilerParams(vmem_limit_bytes=SMALL_VMEM),
        )(*operands)

    def placed(kernel, first_core):
        return lambda *refs: kernel(first_core, here(), *refs)

    def scan(part, flags, reverse):
        kernel = functools.partial(scan_kernel, reverse)
        return small(kernel, state(rows, SLICE, HEAD_DIM), part, flags)

    def combine(first_core, mine, received, depth):
        kernel = placed(combine_kernel, first_core)
        return small(kernel, state(rows, depth, HEAD_DIM), mine, received)

    def spread(first_core, entering, mine, received):
        kernel = placed(spread_kernel, first_core)
        shape = state(rows * SLICE, HEAD_DIM)
        own, other = small(kernel, [shape, shape], entering, mine, received)
        return own, sibling(other)

    received = sibling(theirs)
    flags = exchange(combine(0, mine, received, SLICE + 8))
    entering = exchange(scan(flags, flags, False))
    local = call(
        placeless(functools.partial(local_kernel, per_step)),
        [wide] * 3,
        wide,
        tall,
        2 * 512,
        10,
    )(queries, keys, values)

    entering, local = lax.optimization_barrier((entering, local))
    prefix = spread(0, entering, mine, received)

    attended, sums = stream(
        functools.partial(attended_kernel, heads),
        [queries, local, cotangent], [gain, *prefix], [tall], [state(2, tokens)], HEAD_DIM, 12,
    )

    count = lax.axis_size("head")
    all_sums = [sums] + [
        lax.ppermute(sums, "head", [(i, (i + step) % count) for i in range(count)])
        for step in range(1, count)
    ]
    normed, grad_out, theirs, mine = stream(
        functools.partial(norm_kernel, heads, features),
        [attended, queries, cotangent], [gain, *all_sums], [narrow, narrow], parted, HEAD_DIM, 13,
        clear_state, split_state, [total_rows],
    )

    received = sibling(theirs)
    gathered = exchange(combine(1, mine, received, SLICE))
    grad_q, key_part = call(
        functools.partial(back_kernel, per_step),
        [wide] * 4 + [halves, halves],
        [wide] * 2,
        [narrow, tall],
        3 * 512 + HEAD_DIM,
        14,
        [pltpu.VMEM((tokens, step_cols), F32)],
    )(queries, keys, values, grad_out, *prefix)
    gathered, grad_q, key_part = lax.optimization_barrier((gathered, grad_q, key_part))
    entering = exchange(scan(gathered, flags, True))
    value_part = call(
        placeless(functools.partial(value_kernel, per_step)),
        [wide] * 3,
        wide,
        tall,
        2 * 512,
        10,
    )(queries, keys, grad_out)
    entering, value_part = lax.optimization_barrier((entering, value_part))
    suffix = spread(1, entering, mine, received)

    grad_k, grad_v = stream(
        functools.partial(finish_kernel, heads),
        [keys, values, key_part, value_part], [*suffix], [narrow, narrow], [], 2 * HEAD_DIM, 16,
    )
    return normed, grad_q, grad_k, grad_v


def solution(mesh):
    wide = P("seq", "head")
    return jax.shard_map(
        on_device,
        mesh=mesh,
        in_specs=(wide, wide, wide, wide, P("head"), P("seq")),
        out_specs=(wide, wide, wide, wide),
        check_vma=False,
    )
```

```python
import functools

import jax
import jax.numpy as jnp
from jax import lax
from jax.experimental import pallas as pl
from jax.experimental.pallas import tpu as pltpu
from jax.sharding import PartitionSpec as P

HEAD_DIM = 128
UNIT = 256
SLICE = 16
ROWS = 256
VMEM = 58 * 1024 * 1024
ROW_VMEM = 58 * 1024 * 1024
SMALL_VMEM = 8 * 1024 * 1024
epsilon = 1e-06

F32 = jnp.float32
BF16 = jnp.bfloat16


def dot(left, right, contract):
    return lax.dot_general(
        left, right, ((contract[0:1], contract[1:2]), ((), ())), preferred_element_type=F32
    )


def unit(index):
    return slice(index * UNIT, (index + 1) * UNIT)


def columns(index):
    return slice(index * HEAD_DIM, (index + 1) * HEAD_DIM)


def causal(later_dim=0):
    later = lax.broadcasted_iota(jnp.int32, (UNIT, UNIT), later_dim)
    return later >= lax.broadcasted_iota(jnp.int32, (UNIT, UNIT), 1 - later_dim)


def tile_mask(doc_ref, later, earlier):
    if later == earlier:
        return causal()
    return jnp.full((UNIT, UNIT), doc_ref[later * UNIT] == doc_ref[earlier * UNIT])


def masked_rows(keep, rows):
    return jnp.where(jnp.full(rows.shape, keep), rows, jnp.zeros_like(rows))


def column_of(row):
    return jnp.transpose(jnp.broadcast_to(row, (HEAD_DIM, row.shape[1])))


def add_state(total, left_ref, right_ref, keep, heads):
    for h in range(heads):
        left = masked_rows(keep, left_ref[:, columns(h)])
        total[columns(h), :] += dot(left, right_ref[:, columns(h)], (0, 0))


def split_state(total, doc_ref, place_ref, theirs_ref, mine_ref):
    rows = total.shape[0] // (2 * SLICE)
    flag = jnp.where(doc_ref[doc_ref.shape[0] - 1] >= place_ref[0], 0.0, 1.0).astype(F32)
    low = total[: rows * SLICE, :].reshape(rows, SLICE, HEAD_DIM)
    high = total[rows * SLICE :, :].reshape(rows, SLICE, HEAD_DIM)
    is_low = jnp.full(low.shape, place_ref[1] == 0)
    mine_ref[0:rows] = jnp.where(is_low, low, high)
    theirs_ref[0:rows] = jnp.where(is_low, high, low)
    mine_ref[rows] = jnp.full((SLICE, HEAD_DIM), flag)
    theirs_ref[rows] = jnp.full((SLICE, HEAD_DIM), flag)


def streamed(kernel, before, after, ins, outs):
    def body(doc_ref, place_ref, *refs):
        sources, rest = refs[:ins], refs[ins:]
        targets, rest = rest[-outs:] if outs else (), rest[: len(rest) - outs] if outs else rest
        buffers, sems = rest[-1 - ins - outs : -1], rest[-1]
        rest = rest[: -1 - ins - outs]
        bands = doc_ref.shape[0] // ROWS

        def copy(k, i):
            rows = pl.ds(i * ROWS, ROWS)
            if k < ins:
                ends = sources[k].at[rows], buffers[k].at[rows]
            else:
                ends = buffers[k].at[rows], targets[k - ins].at[rows]
            return pltpu.make_async_copy(*ends, sems.at[k, i])

        for i in range(bands):
            for k in range(ins):
                copy(k, i).start()
        if before is not None:
            before(doc_ref, place_ref, *rest)
        for i in range(bands):
            for k in range(ins):
                copy(k, i).wait()
            views = [b.at[pl.ds(i * ROWS, ROWS)] for b in buffers]
            kernel(i, doc_ref, place_ref, *views, *rest)
            for k in range(ins, ins + outs):
                copy(k, i).start()
        if after is not None:
            after(doc_ref, place_ref, *rest)
        for i in range(bands):
            for k in range(ins, ins + outs):
                copy(k, i).wait()

    return body


def add_state(total, left_ref, right_ref, keep, heads):
    for h in range(heads):
        left = masked_rows(keep, left_ref[:, columns(h)])
        total[columns(h), :] += dot(left, right_ref[:, columns(h)], (0, 0))


def split_state(doc_ref, place_ref, *refs):
    theirs_ref, mine_ref, total = refs[-3:]
    rows = total.shape[0] // (2 * SLICE)
    flag = jnp.where(doc_ref[doc_ref.shape[0] - 1] >= place_ref[0], 0.0, 1.0).astype(F32)
    low = total[: rows * SLICE, :].reshape(rows, SLICE, HEAD_DIM)
    high = total[rows * SLICE :, :].reshape(rows, SLICE, HEAD_DIM)
    is_low = jnp.full(low.shape, place_ref[1] == 0)
    mine_ref[0:rows] = jnp.where(is_low, low, high)
    theirs_ref[0:rows] = jnp.where(is_low, high, low)
    mine_ref[rows] = jnp.full((SLICE, HEAD_DIM), flag)
    theirs_ref[rows] = jnp.full((SLICE, HEAD_DIM), flag)


def clear_state(doc_ref, place_ref, *refs):
    refs[-1][...] = jnp.zeros_like(refs[-1])


def tail_kernel(heads, i, doc_ref, place_ref, key_ref, value_ref, theirs_ref, mine_ref, total):
    keep = doc_ref[i * ROWS] == doc_ref[doc_ref.shape[0] - 1]
    add_state(total, key_ref, value_ref, keep, heads)


def combine_kernel(first_core, place_ref, mine_ref, theirs_ref, total_ref):
    rows = total_ref.shape[0]
    my_flag, their_flag = mine_ref[rows, 0:1, :], theirs_ref[rows, 0:1, :]
    first = jnp.full((SLICE, HEAD_DIM), place_ref[1] == first_core)
    for i in range(rows):
        mine, theirs = mine_ref[i], theirs_ref[i]
        total_ref[i, 0:SLICE, :] = jnp.where(
            first, theirs + their_flag * mine, mine + my_flag * theirs
        )
    if total_ref.shape[1] > SLICE:
        total_ref[:, SLICE:, :] = jnp.broadcast_to(my_flag * their_flag, (rows, 8, HEAD_DIM))


def spread_kernel(first_core, place_ref, entering_ref, mine_ref, theirs_ref, own_ref, other_ref):
    rows = entering_ref.shape[0]
    my_flag, their_flag = mine_ref[rows, 0:1, :], theirs_ref[rows, 0:1, :]
    first = jnp.full((SLICE, HEAD_DIM), place_ref[1] == first_core)
    for i in range(rows):
        entering = entering_ref[i]
        place = slice(i * SLICE, (i + 1) * SLICE)
        own_ref[place, :] = jnp.where(first, entering, theirs_ref[i] + their_flag * entering)
        other_ref[place, :] = jnp.where(first, mine_ref[i] + my_flag * entering, entering)


def scan_kernel(reverse, part_ref, flag_ref, state_ref):
    count = part_ref.shape[0]
    carry = jnp.zeros((SLICE, HEAD_DIM), F32)
    for step in range(count):
        b = count - 1 - step if reverse else step
        state_ref[b] = carry
        carry = part_ref[b, 0:SLICE, :] + flag_ref[b, SLICE : SLICE + 1, :] * carry


def picked(place_ref, mine_ref, theirs_ref, is_mine, h):
    rows = slice(h * HEAD_DIM, (h + 1) * HEAD_DIM)
    keep = jnp.full((HEAD_DIM, HEAD_DIM), is_mine)
    return jnp.where(keep, mine_ref[rows, :], theirs_ref[rows, :]).astype(BF16)


def pick(place_ref, mine_ref, theirs_ref, h):
    is_mine = pl.program_id(0) // (pl.num_programs(0) // 2) == place_ref[1]
    return picked(place_ref, mine_ref, theirs_ref, is_mine, h)


def pick_head(place_ref, mine_ref, theirs_ref, heads, h):
    half = heads // 2
    return picked(place_ref, mine_ref, theirs_ref, place_ref[1] == h // half, h % half)


def attended_kernel(heads, i, doc_ref, place_ref, query_ref, local_ref, cotangent_ref, out_ref,
                    gain_ref, mine_ref, theirs_ref, sums_ref):
    carried = doc_ref[i * ROWS] < place_ref[0]
    squares = jnp.zeros((ROWS, HEAD_DIM), F32)
    crosses = jnp.zeros((ROWS, HEAD_DIM), F32)
    for h in range(heads):
        query = masked_rows(carried, query_ref[:, columns(h)])
        prefix = pick_head(place_ref, mine_ref, theirs_ref, heads, h)
        out = local_ref[:, columns(h)] + dot(query, prefix, (1, 0))
        out_ref[:, columns(h)] = out
        scaled = gain_ref[0:1, columns(h)] * cotangent_ref[:, columns(h)].astype(F32)
        squares += out * out
        crosses += scaled * out
    band = slice(i * ROWS, (i + 1) * ROWS)
    sums_ref[0:1, band] = jnp.sum(jnp.transpose(squares), axis=0, keepdims=True)
    sums_ref[1:2, band] = jnp.sum(jnp.transpose(crosses), axis=0, keepdims=True)


def norm_kernel(heads, features, i, doc_ref, place_ref, out_ref, query_ref, cotangent_ref,
                normed_ref, grad_ref, gain_ref, sums_ref, sums1_ref, sums2_ref, sums3_ref,
                theirs_ref, mine_ref, total):
    band = slice(i * ROWS, (i + 1) * ROWS)
    sums = sums_ref[:, band] + sums1_ref[:, band] + sums2_ref[:, band] + sums3_ref[:, band]
    inv_row = lax.rsqrt(sums[0:1] / features + epsilon)
    inv = column_of(inv_row)
    factor = column_of(inv_row * inv_row * sums[1:2] / features)
    for h in range(heads):
        out = out_ref[:, columns(h)]
        gain = gain_ref[0:1, columns(h)]
        normed_ref[:, columns(h)] = (out * inv * gain).astype(BF16)
        scaled = gain * cotangent_ref[:, columns(h)].astype(F32)
        grad_ref[:, columns(h)] = (inv * (scaled - out * factor)).astype(BF16)
    add_state(total, query_ref, grad_ref, doc_ref[i * ROWS] < place_ref[0], heads)


def rows_from(unit_index):
    return slice(unit_index * UNIT, None)


def lower_scores(doc_ref, left_ref, right_ref, s, h):
    scores = dot(left_ref[rows_from(s), columns(h)], right_ref[unit(s), columns(h)], (1, 1))
    units = left_ref.shape[0] // UNIT
    tiles = [
        jnp.where(tile_mask(doc_ref, t, s), scores[unit(t - s)], 0.0).astype(BF16)
        for t in range(s, units)
    ]
    return jnp.concatenate(tiles, 0)


def upper_scores(doc_ref, left_ref, right_ref, s, h):
    scores = dot(left_ref[unit(s), columns(h)], right_ref[rows_from(s), columns(h)], (1, 1))
    tiles = []
    for t in range(s, right_ref.shape[0] // UNIT):
        mask = tile_mask(doc_ref, t, s) if t > s else causal(1)
        tiles.append(jnp.where(mask, scores[:, unit(t - s)], 0.0).astype(BF16))
    return jnp.concatenate(tiles, 1)


def local_kernel(heads, doc_ref, query_ref, key_ref, value_ref, out_ref):
    for h in range(heads):
        for s in range(query_ref.shape[0] // UNIT):
            attend = lower_scores(doc_ref, query_ref, key_ref, s, h)
            part = dot(attend, value_ref[unit(s), columns(h)], (1, 0))
            if s == 0:
                out_ref[:, columns(h)] = part
            else:
                out_ref[rows_from(s), columns(h)] += part


def back_kernel(heads, doc_ref, place_ref, key_ref, value_ref, grad_ref, mine_ref, theirs_ref,
                grad_q_ref, grad_q):
    units = key_ref.shape[0] // UNIT
    for h in range(heads):
        prefix = pick(place_ref, mine_ref, theirs_ref, h)
        for t in range(units):
            carried = masked_rows(doc_ref[t * UNIT] < place_ref[0], grad_ref[unit(t), columns(h)])
            grad_q[unit(t), columns(h)] = dot(carried, prefix, (1, 1))
        for s in range(units):
            backs = lower_scores(doc_ref, grad_ref, value_ref, s, h)
            grad_q[rows_from(s), columns(h)] += dot(backs, key_ref[unit(s), columns(h)], (1, 0))
        grad_q_ref[:, columns(h)] = grad_q[:, columns(h)].astype(BF16)


def parts_kernel(heads, doc_ref, query_ref, key_ref, value_ref, grad_ref, key_part_ref,
                 value_part_ref):
    for h in range(heads):
        for s in range(query_ref.shape[0] // UNIT):
            attend = upper_scores(doc_ref, key_ref, query_ref, s, h)
            value_part_ref[unit(s), columns(h)] = dot(
                attend, grad_ref[rows_from(s), columns(h)], (1, 0)
            )
            backs = upper_scores(doc_ref, value_ref, grad_ref, s, h)
            key_part_ref[unit(s), columns(h)] = dot(
                backs, query_ref[rows_from(s), columns(h)], (1, 0)
            )


def finish_kernel(heads, i, doc_ref, place_ref, key_ref, value_ref, key_part_ref,
                  value_part_ref, grad_k_ref, grad_v_ref, mine_ref, theirs_ref):
    closing = doc_ref[i * ROWS] == doc_ref[doc_ref.shape[0] - 1]
    for h in range(heads):
        suffix = pick_head(place_ref, mine_ref, theirs_ref, heads, h)
        value = masked_rows(closing, value_ref[:, columns(h)])
        grad_k = key_part_ref[:, columns(h)] + dot(value, suffix, (1, 1))
        grad_k_ref[:, columns(h)] = grad_k.astype(BF16)
        key = masked_rows(closing, key_ref[:, columns(h)])
        grad_v = value_part_ref[:, columns(h)] + dot(key, suffix, (1, 0))
        grad_v_ref[:, columns(h)] = grad_v.astype(BF16)


def on_device(queries, keys, values, cotangent, norm_gain, doc_start):
    tokens, width = queries.shape
    blocks = lax.axis_size("seq")
    chips = blocks // 2
    heads = width // HEAD_DIM
    per_step = 2
    steps = heads // per_step
    features = width * lax.axis_size("head")
    gain = norm_gain.reshape(1, width)

    def here():
        block = lax.axis_index("seq")
        return block * tokens, lax.rem(block, 2)

    step_cols = per_step * HEAD_DIM
    docs = pl.BlockSpec(memory_space=pltpu.SMEM)

    wide = pl.BlockSpec((tokens, step_cols), lambda i: (0, i))
    anywhere = pl.BlockSpec(memory_space=pl.ANY)
    vmem = pl.BlockSpec(memory_space=pltpu.VMEM)

    def stream(kernel, arrays, operands, wide_outs, outs, products, traffic, before=None,
               after=None, scratch=()):
        ins, count = len(arrays), len(wide_outs)
        inner = streamed(kernel, before, after, ins, count)

        def body(doc_ref, *refs):
            front, rest = refs[: ins + len(operands)], refs[ins + len(operands) :]
            big, small_outs = rest[:count], rest[count : count + len(outs)]
            extra = rest[count + len(outs) :]
            own, buffers = extra[: len(scratch)], extra[len(scratch) :]
            inner(doc_ref, here(), *front, *small_outs, *own, *buffers, *big)

        return pl.pallas_call(
            body,
            in_specs=[docs] + [anywhere] * ins + [vmem] * len(operands),
            out_specs=[anywhere] * count + [vmem] * len(outs),
            out_shape=list(wide_outs) + list(outs),
            scratch_shapes=list(scratch)
            + [pltpu.VMEM(a.shape, a.dtype) for a in list(arrays) + list(wide_outs)]
            + [pltpu.SemaphoreType.DMA((ins + count, tokens // ROWS))],
            cost_estimate=pl.CostEstimate(
                flops=2 * products * tokens * width,
                bytes_accessed=traffic * tokens * width,
                transcendentals=0,
            ),
            compiler_params=pltpu.CompilerParams(vmem_limit_bytes=ROW_VMEM),
        )(doc_start, *arrays, *operands)

    halves = pl.BlockSpec((step_cols, HEAD_DIM), lambda i: (i % 2, 0))
    tall = jax.ShapeDtypeStruct((tokens, width), F32)
    narrow = jax.ShapeDtypeStruct((tokens, width), BF16)

    def state(*shape):
        return jax.ShapeDtypeStruct(shape, F32)

    def call(kernel, ins, outs, shapes, products, arrays, scratch=()):
        def body(doc_ref, *refs):
            kernel(doc_ref, here(), *refs)

        return functools.partial(
            pl.pallas_call(
                body,
                grid=(steps,),
                in_specs=[docs] + ins,
                out_specs=outs,
                scratch_shapes=list(scratch),
                out_shape=shapes,
                cost_estimate=pl.CostEstimate(
                    flops=2 * products * tokens * width,
                    bytes_accessed=arrays * tokens * width,
                    transcendentals=0,
                ),
                compiler_params=pltpu.CompilerParams(vmem_limit_bytes=VMEM),
            ),
            doc_start,
        )

    def placeless(kernel):
        return lambda doc_ref, place_ref, *refs: kernel(doc_ref, *refs)

    rows = heads // 2 * HEAD_DIM // SLICE
    total_rows = pltpu.VMEM((width, HEAD_DIM), F32)
    parted = [state(rows + 1, SLICE, HEAD_DIM)] * 2
    theirs, mine = stream(
        functools.partial(tail_kernel, heads),
        [keys, values], [], [], parted, HEAD_DIM, 5, clear_state, split_state, [total_rows],
    )

    def sibling(data):
        return lax.ppermute(data, "seq", [(i, i ^ 1) for i in range(blocks)])

    groups = [[2 * chip + c for chip in range(chips)] for c in range(2)]

    def exchange(data):
        return lax.all_to_all(data, "seq", 0, 0, axis_index_groups=groups)

    def small(kernel, shapes, *operands):
        return pl.pallas_call(
            kernel,
            out_shape=shapes,
            compiler_params=pltpu.CompilerParams(vmem_limit_bytes=SMALL_VMEM),
        )(*operands)

    def placed(kernel, first_core):
        return lambda *refs: kernel(first_core, here(), *refs)

    def scan(part, flags, reverse):
        kernel = functools.partial(scan_kernel, reverse)
        return small(kernel, state(rows, SLICE, HEAD_DIM), part, flags)

    def combine(first_core, mine, received, depth):
        kernel = placed(combine_kernel, first_core)
        return small(kernel, state(rows, depth, HEAD_DIM), mine, received)

    def spread(first_core, entering, mine, received):
        kernel = placed(spread_kernel, first_core)
        shape = state(rows * SLICE, HEAD_DIM)
        own, other = small(kernel, [shape, shape], entering, mine, received)
        return own, sibling(other)

    received = sibling(theirs)
    flags = exchange(combine(0, mine, received, SLICE + 8))
    entering = exchange(scan(flags, flags, False))
    local = call(
        placeless(functools.partial(local_kernel, per_step)),
        [wide] * 3,
        wide,
        tall,
        2 * 512,
        10,
    )(queries, keys, values)

    entering, local = lax.optimization_barrier((entering, local))
    prefix = spread(0, entering, mine, received)

    attended, sums = stream(
        functools.partial(attended_kernel, heads),
        [queries, local, cotangent], [gain, *prefix], [tall], [state(2, tokens)], HEAD_DIM, 12,
    )

    count = lax.axis_size("head")
    all_sums = [sums] + [
        lax.ppermute(sums, "head", [(i, (i + step) % count) for i in range(count)])
        for step in range(1, count)
    ]
    normed, grad_out, theirs, mine = stream(
        functools.partial(norm_kernel, heads, features),
        [attended, queries, cotangent], [gain, *all_sums], [narrow, narrow], parted, HEAD_DIM, 13,
        clear_state, split_state, [total_rows],
    )

    received = sibling(theirs)
    gathered = exchange(combine(1, mine, received, SLICE))
    (grad_q,) = call(
        functools.partial(back_kernel, per_step),
        [wide] * 3 + [halves, halves],
        [wide],
        [narrow],
        2 * 512 + HEAD_DIM,
        8,
        [pltpu.VMEM((tokens, step_cols), F32)],
    )(keys, values, grad_out, *prefix)
    gathered, grad_q = lax.optimization_barrier((gathered, grad_q))
    entering = exchange(scan(gathered, flags, True))
    parts = call(
        placeless(functools.partial(parts_kernel, per_step)),
        [wide] * 4,
        [wide] * 2,
        [tall, tall],
        4 * 512,
        16,
    )(queries, keys, values, grad_out)
    entering, key_part, value_part = lax.optimization_barrier((entering, *parts))
    suffix = spread(1, entering, mine, received)

    grad_k, grad_v = stream(
        functools.partial(finish_kernel, heads),
        [keys, values, key_part, value_part], [*suffix], [narrow, narrow], [], 2 * HEAD_DIM, 16,
    )
    return normed, grad_q, grad_k, grad_v


def solution(mesh):
    wide = P("seq", "head")
    return jax.shard_map(
        on_device,
        mesh=mesh,
        in_specs=(wide, wide, wide, wide, P("head"), P("seq")),
        out_specs=(wide, wide, wide, wide),
        check_vma=False,
    )
```
